32 devices in a mesh: groups: 2 (over x), blk: 16 (over z, y, core).
Axes of the slice: x: 2, y: 2, z: 4, core: 2. Of those that a mesh axis runs over, the one named last changes fastest.
Arguments:
- in_factors: bfloat16 [32768, 16, 64], P(('groups', 'blk')), parts along dimension 0, may hold values from -6 to 6
- out_factors: bfloat16 [32768, 16, 64], P(('groups', 'blk')), parts along dimension 0, may hold values from -6 to 6
- token_counts: int32 [32768], P(('groups', 'blk')), parts along dimension 0, may hold values from 1 to 16, as said below
- train_cluster: int32 [32768], P(('groups', 'blk')), parts along dimension 0, may hold values from 0 to 3
- queries: bfloat16 [4096, 4096], P(('groups', 'blk')), parts along dimension 0, may hold values from -6 to 6
- query_cluster: int32 [4096], P('groups'), parts along dimension 0, may hold values from 0 to 3
- pair_mask: int32 [256, 9], P(('groups', 'blk')), parts along dimension 0, may hold values from 0 to 1
Outputs:
- train_score: float32 [32768], P(('groups', 'blk')), parts along dimension 0
- query_score: float32 [4096], P(('groups', 'blk')), parts along dimension 0
The draws below stay inside these ranges and needn't reach their ends.
There are 2 independent parts, one for each index of `groups`. The reference program is written for one: setup_inputs(seed, part) draws one part's arguments, and reference() takes and returns one part's arrays. A program takes and returns all parts, laid end to end along the dimension named above; each array names one. Nothing has to cross between parts.
Inputs may be any that keep to these rules, and one draw needn't show every extreme that they name: `token_counts`: each train row has at least one counted token, and some row reaches 16.
All inputs are finite; a program needn't handle non-finite values.
Results may differ from the reference program's by a relative error of at most 0.00046.
Values may be sent and summed in bfloat16 or wider, within the bound.
A program may use at most 128 MiB of HBM per device.

```python
import jax
import jax.numpy as jnp
from jax import lax

RIN = 64
ROUT = 64
TILE = 128
TR_DEV = 1024
LEN = 16
REACH = 4
BAND = 9
TRAIN = 16384
QUERIES = 2048
TTILES = 128
N_BLK = 16


def draw_token_counts(key, part):
    key = jax.random.fold_in(key, 11)
    counts = jax.random.randint(key, (TRAIN,), 1, LEN + 1)
    marked = jnp.arange(TRAIN, dtype=jnp.int32) % 64 == 0
    return jnp.where(marked, LEN, counts).astype(jnp.int32)


def draw_pair_mask(key, part):
    key = jax.random.fold_in(key, 23)
    level_key, bits_key = jax.random.split(key)
    nblocks = TRAIN // TR_DEV
    levels = jax.random.randint(level_key, (nblocks, 1, 1), 1, 5)
    bits = jax.random.randint(bits_key, (nblocks, TR_DEV // TILE, BAND), 0, 4)
    return (bits < levels).astype(jnp.int32).reshape(TTILES, BAND)


def plant(array, own_key, low, top_value):
    place = [jax.random.randint(jax.random.fold_in(own_key, axis), (), 0, length) for axis, length in enumerate(array.shape)]
    longest = array.shape.index(max(array.shape))
    beside = place[:longest] + [(place[longest] + 1) % array.shape[longest]] + place[longest + 1:]
    return array.at[tuple(place)].set(low).at[tuple(beside)].set(top_value)


def block_levels(key, dims, cuts, smallest, largest):
    def one(position, shards_of):
        heights = jax.random.uniform(jax.random.fold_in(jax.random.fold_in(key, 6), position), (shards_of,), jnp.float32, smallest / len(cuts), largest / len(cuts))
        return jnp.repeat(jnp.exp(heights), dims[position] // shards_of).reshape((-1,) + (1,) * (len(dims) - position - 1))

    level = one(*cuts[0])
    for cut in cuts[1:]:
        level = level * one(*cut)
    return level


def normal_values(own_key, dims, scale, reach, cuts=(), held_as=jnp.bfloat16):
    drawn = jax.random.normal(own_key, dims, jnp.float32) * scale
    if len(cuts) > 0:
        drawn = block_levels(own_key, dims, cuts, -0.22, 0.18) * drawn
    return jnp.clip(drawn, min=-reach, max=reach).astype(held_as)


def setup_inputs(seed: int = 0, part: int = 0) -> dict:
    seeds = jax.random.split(jax.random.key(seed), 8)
    part_splits = jax.random.split(jax.random.fold_in(seeds[7], part), 8)
    in_factors = normal_values(part_splits[0], (TRAIN, LEN, RIN), 1.0, 6.0, ((0, 16),))
    out_factors = normal_values(part_splits[1], (TRAIN, LEN, ROUT), 1.0, 6.0, ((0, 16),))
    token_counts = draw_token_counts(jax.random.fold_in(jax.random.fold_in(seeds[7], part), 71), part)
    train_cluster = plant(jax.random.randint(part_splits[3], (TRAIN,), 0, 4), jax.random.fold_in(part_splits[3], 1), 0, 3).astype(jnp.int32)
    queries = normal_values(part_splits[4], (QUERIES, RIN * ROUT), 1.0, 6.0, ((0, 16),))
    query_cluster = plant(jax.random.randint(part_splits[5], (QUERIES,), 0, 4), jax.random.fold_in(part_splits[5], 1), 0, 3).astype(jnp.int32)
    pair_mask = draw_pair_mask(jax.random.fold_in(jax.random.fold_in(seeds[7], part), 71), part)
    return {"in_factors": in_factors, "out_factors": out_factors, "token_counts": token_counts, "train_cluster": train_cluster, "queries": queries, "query_cluster": query_cluster, "pair_mask": pair_mask}


def reference(in_factors, out_factors, token_counts, train_cluster, queries, query_cluster, pair_mask):
    nblocks = N_BLK
    tiles_dev = TR_DEV // TILE
    width = RIN * ROUT
    inv = 1.0 / (width ** 0.5)
    in_blocks = in_factors.reshape(nblocks, TR_DEV, LEN, RIN)
    out_blocks = out_factors.reshape(nblocks, TR_DEV, LEN, ROUT)
    count_blocks = token_counts.reshape(nblocks, TR_DEV)
    tclus_blocks = train_cluster.reshape(nblocks, TR_DEV)
    query_blocks = queries.reshape(nblocks, TILE, width)
    qclus_blocks = query_cluster.reshape(nblocks, TILE)
    mask_blocks = pair_mask.reshape(nblocks, tiles_dev, BAND)

    def per_block(qsum, index):
        left = lax.dynamic_index_in_dim(in_blocks, index, 0, keepdims=False).astype(jnp.float32)
        right = lax.dynamic_index_in_dim(out_blocks, index, 0, keepdims=False).astype(jnp.float32)
        counts = lax.dynamic_index_in_dim(count_blocks, index, 0, keepdims=False)
        tclus = lax.dynamic_index_in_dim(tclus_blocks, index, 0, keepdims=False)
        masks = lax.dynamic_index_in_dim(mask_blocks, index, 0, keepdims=False)
        live = (jnp.arange(LEN, dtype=jnp.int32)[None, :] < counts[:, None]).astype(jnp.float32)
        left = left * live[:, :, None]
        sketch = jnp.einsum("rti,rto->rio", left, right).reshape(TR_DEV, width).astype(jnp.bfloat16)
        tsum = jnp.zeros((TR_DEV,), jnp.float32)
        for column in range(BAND):
            source = ((index + column - REACH) % nblocks).astype(jnp.int32)
            qrows = lax.dynamic_index_in_dim(query_blocks, source, 0, keepdims=False)
            qclus = lax.dynamic_index_in_dim(qclus_blocks, source, 0, keepdims=False)
            scores = jnp.dot(sketch, qrows.T, preferred_element_type=jnp.float32) * inv
            rowmask = jnp.repeat(masks[:, column], TILE).astype(jnp.float32)
            weight = (tclus[:, None] == qclus[None, :]).astype(jnp.float32) * rowmask[:, None]
            weighted = weight * jnp.maximum(scores, 0.0)
            tsum = tsum + jnp.sum(weighted, axis=1)
            qsum = qsum.at[source].add(jnp.sum(weighted, axis=0))
        return qsum, tsum

    start = jnp.zeros((nblocks, TILE), jnp.float32)
    qsum, tsums = lax.scan(per_block, start, jnp.arange(nblocks, dtype=jnp.int32))
    return tsums.reshape(-1) / 32.0, qsum.reshape(-1) / 32.0
```

```python
import jax
import jax.numpy as jnp
from jax import lax
from jax.experimental import pallas as pl
from jax.experimental.pallas import tpu as pltpu
from jax.sharding import PartitionSpec as P

HALVES = 2
PLANE = 4
GROUP = 4

OWN, CORE, SIDE, CORE_SIDE, FIRST, SECOND, DIAG, CORE_DIAG, CORE_PLANE = range(9)
SLOTS = 9


def kernel(
    in_hbm, out_hbm, counts_ref, tclus_ref, q_hbm, qclus_ref, mask_ref,
    train_ref, query_ref,
    in_raw, out_raw, in_f32, out_f32, sketch, blocks, qacc, tacc, qout, qin,
    load_sem, own_sem, send_sem, recv_sem, back_send, back_recv,
):
    n = lax.axis_size("blk")
    b = lax.axis_index("blk")
    place = lax.rem(b, PLANE)
    side = place // 2
    core = lax.rem(place, 2)
    slots, rin, rows = in_f32.shape
    rout = out_f32.shape[1]
    tile = query_ref.shape[1]
    band = mask_ref.shape[1]
    reach = (band - 1) // 2
    width = rin * rout
    piece = tile // HALVES
    scale = 1.0 / width**0.5 / 32.0

    to_core = b + 1 - 2 * core
    to_side = b + 2 - 4 * side
    above = lax.rem(b + PLANE, n)
    below = lax.rem(b + n - PLANE, n)
    to_first = side * above + (1 - side) * below
    to_second = side * below + (1 - side) * above
    offsets = {
        OWN: 0,
        CORE: 1 - 2 * core,
        SIDE: 2 - 4 * side,
        CORE_SIDE: 3 - 2 * place,
        FIRST: 4 - 8 * side,
        SECOND: 8 * side - 4,
        DIAG: 4 * side - 2,
        CORE_DIAG: 8 * side - 1 - 2 * place,
        CORE_PLANE: 6 * core - 3,
    }

    load_in = pltpu.make_async_copy(in_hbm, in_raw, load_sem.at[0])
    load_out = pltpu.make_async_copy(out_hbm, out_raw, load_sem.at[1])
    load_in.start()
    load_out.start()

    barrier = pltpu.get_barrier_semaphore()
    for step in range(1, reach + 1):
        for other in (lax.rem(b + step, n), lax.rem(b + n - step, n)):
            pl.semaphore_signal(
                barrier, inc=1, device_id={"blk": other}, device_id_type=pl.DeviceIdType.MESH
            )
    pl.semaphore_wait(barrier, 2 * reach)

    def own(h):
        return q_hbm.at[pl.ds(h * piece, piece), :]

    def send(src, slot, h, device):
        return pltpu.make_async_remote_copy(
            src_ref=src,
            dst_ref=blocks.at[h, slot],
            send_sem=send_sem.at[slot, h],
            recv_sem=recv_sem.at[slot, h],
            device_id={"blk": device},
            device_id_type=pl.DeviceIdType.MESH,
        )

    halves = range(HALVES)
    first = [send(own(h), FIRST, h, to_first) for h in halves]
    aside = [send(own(h), SIDE, h, to_side) for h in halves]
    twin = [send(own(h), CORE, h, to_core) for h in halves]
    second = [send(own(h), SECOND, h, to_second) for h in halves]
    diag = [send(blocks.at[h, FIRST], DIAG, h, to_side) for h in halves]
    twin_side = [send(blocks.at[h, SIDE], CORE_SIDE, h, to_core) for h in halves]
    twin_diag = [send(blocks.at[h, DIAG], CORE_DIAG, h, to_core) for h in halves]
    plane_first = [send(blocks.at[h, FIRST], CORE_PLANE, h, to_core) for h in halves]
    plane_second = [send(blocks.at[h, SECOND], CORE_PLANE, h, to_core) for h in halves]
    mine = [pltpu.make_async_copy(own(h), blocks.at[h, OWN], own_sem.at[h]) for h in halves]
    for h in halves:
        first[h].start()
        aside[h].start()
    for h in halves:
        twin[h].start()
        mine[h].start()

    load_in.wait()
    load_out.wait()
    counts = counts_ref[...]

    @pl.loop(0, slots)
    def _(t):
        live = counts > t
        value = in_raw[t].astype(jnp.float32)
        in_f32[t] = jnp.where(live, value, 0.0)
        out_f32[t] = out_raw[t].astype(jnp.float32)

    @pl.loop(0, rows // 128)
    def _(chunk):
        lanes = pl.ds(pl.multiple_of(chunk * 128, 128), 128)

        @pl.loop(0, rin // 8)
        def _(group):
            eight = pl.ds(pl.multiple_of(group * 8, 8), 8)
            for low in range(0, 8, GROUP):
                sums = [None] * GROUP
                for t in range(slots):
                    right = out_f32[t, :, lanes]
                    left = in_f32[t, eight, lanes]
                    for g in range(GROUP):
                        row = left[low + g : low + g + 1]
                        term = row * right
                        sums[g] = term if t == 0 else sums[g] + term
                for g in range(GROUP):
                    at = pl.multiple_of(group * (8 * rout) + (low + g) * rout, rout)
                    sketch[pl.ds(at, rout), lanes] = sums[g].astype(jnp.bfloat16)

    for h in halves:
        first[h].wait_send()
    for h in halves:
        second[h].start()
    for h in halves:
        first[h].wait_recv()
        diag[h].start()

        @pl.when(side == core)
        def _(h=h):
            plane_first[h].start()

        aside[h].wait_recv()
        twin_side[h].start()

    tacc[...] = jnp.zeros_like(tacc)
    qacc[...] = jnp.zeros_like(qacc)

    def score(h, low, high):
        clusters = []
        for slot in range(low, high):
            source = lax.rem(b + offsets[slot] + n, n)
            row = qclus_ref[source].astype(jnp.float32)
            full = jnp.transpose(jnp.broadcast_to(row, (tile, tile)))
            clusters.append(full[h * piece : (h + 1) * piece])

        @pl.loop(0, rows // 256)
        def _(step):
            lanes = pl.ds(pl.multiple_of(step * 256, 256), 256)
            query = blocks[h, low:high].reshape((high - low) * piece, width)
            dots = jnp.dot(query, sketch[:, lanes], preferred_element_type=jnp.float32)
            for part in range(2):
                tile_lanes = pl.ds(pl.multiple_of(step * 256 + part * 128, 128), 128)
                tclus = tclus_ref[:, tile_lanes].astype(jnp.float32)
                total = tacc[:, tile_lanes]
                for i, slot in enumerate(range(low, high)):
                    open_tile = mask_ref[step * 2 + part, offsets[slot] + reach]
                    wanted = jnp.where(open_tile > 0, tclus, -1.0)
                    got = dots[i * piece : (i + 1) * piece, part * 128 : part * 128 + 128]
                    got = jnp.where(clusters[i] == wanted, jnp.maximum(got, 0.0), 0.0)
                    total = total + jnp.sum(got.reshape(piece // 8, 8, 128), axis=0)
                    qacc[slot, h * piece : (h + 1) * piece, :] += got
                tacc[:, tile_lanes] = total

    def back(slot):
        return pltpu.make_async_remote_copy(
            src_ref=qout.at[slot],
            dst_ref=qin.at[offsets[slot] + reach],
            send_sem=back_send.at[slot],
            recv_sem=back_recv.at[offsets[slot] + reach],
            device_id={"blk": lax.rem(b + offsets[slot] + n, n)},
            device_id_type=pl.DeviceIdType.MESH,
        )

    def give_back(low, high):
        for slot in range(low, high):
            qout[slot] = jnp.sum(jnp.transpose(qacc[slot]), axis=0, keepdims=True)
            if slot != OWN:
                back(slot).start()

    for h in halves:
        mine[h].wait()
        twin[h].wait_recv()
        twin_side[h].wait_recv()
        score(h, OWN, SECOND)
    give_back(OWN, SECOND)

    for h in halves:
        second[h].wait_recv()

        @pl.when(side != core)
        def _(h=h):
            plane_second[h].start()

        diag[h].wait_recv()
        twin_diag[h].start()
        twin_diag[h].wait_recv()
        plane_first[h].wait_recv()
        score(h, SECOND, SLOTS)
    give_back(SECOND, SLOTS)

    train_ref[...] = jnp.sum(tacc[...], axis=0, keepdims=True) * scale
    total = qout[OWN]
    for column in range(band):
        if column != reach:
            pltpu.make_async_remote_copy(
                src_ref=qout.at[0],
                dst_ref=qin.at[column],
                send_sem=back_send.at[0],
                recv_sem=back_recv.at[column],
                device_id={"blk": to_core},
                device_id_type=pl.DeviceIdType.MESH,
            ).wait_recv()
            total = total + qin[column]
    query_ref[...] = total * scale

    for h in halves:
        for copy in (aside, twin, second, diag, twin_side, twin_diag, plane_first):
            copy[h].wait_send()
    for slot in range(1, SLOTS):
        back(slot).wait_send()


def per_device(
    in_factors, out_factors, token_counts, train_cluster, queries, query_cluster, pair_mask
):
    rows, slots, rin = in_factors.shape
    rout = out_factors.shape[2]
    tile, width = queries.shape
    nblocks = lax.axis_size("blk")
    band = pair_mask.shape[1]
    piece = tile // HALVES
    vmem = pl.BlockSpec(memory_space=pltpu.VMEM)
    anywhere = pl.BlockSpec(memory_space=pl.ANY)
    train, query = pl.pallas_call(
        kernel,
        out_shape=(
            jax.ShapeDtypeStruct((1, rows), jnp.float32),
            jax.ShapeDtypeStruct((1, tile), jnp.float32),
        ),
        in_specs=[
            anywhere, anywhere, vmem, vmem, anywhere, vmem,
            pl.BlockSpec(memory_space=pltpu.SMEM),
        ],
        out_specs=(vmem, vmem),
        scratch_shapes=[
            pltpu.VMEM((slots, rin, rows), jnp.bfloat16),
            pltpu.VMEM((slots, rout, rows), jnp.bfloat16),
            pltpu.VMEM((slots, rin, rows), jnp.float32),
            pltpu.VMEM((slots, rout, rows), jnp.float32),
            pltpu.VMEM((width, rows), jnp.bfloat16),
            pltpu.VMEM((HALVES, SLOTS, piece, width), jnp.bfloat16),
            pltpu.VMEM((SLOTS, tile, 128), jnp.float32),
            pltpu.VMEM((8, rows), jnp.float32),
            pltpu.VMEM((SLOTS, 1, tile), jnp.float32),
            pltpu.VMEM((band, 1, tile), jnp.float32),
            pltpu.SemaphoreType.DMA((2,)),
            pltpu.SemaphoreType.DMA((HALVES,)),
            pltpu.SemaphoreType.DMA((SLOTS, HALVES)),
            pltpu.SemaphoreType.DMA((SLOTS, HALVES)),
            pltpu.SemaphoreType.DMA((SLOTS,)),
            pltpu.SemaphoreType.DMA((band,)),
        ],
        compiler_params=pltpu.CompilerParams(
            collective_id=0, has_side_effects=True, vmem_limit_bytes=56 * 2**20
        ),
        name="score_blocks",
    )(
        jnp.transpose(in_factors, (1, 2, 0)),
        jnp.transpose(out_factors, (1, 2, 0)),
        token_counts.reshape(1, rows),
        train_cluster.reshape(1, rows),
        queries,
        query_cluster.reshape(nblocks, 1, tile),
        pair_mask,
    )
    return train.reshape(rows), query.reshape(tile)


def solution(mesh):
    placed = (
        P(("groups", "blk"), None, None),
        P(("groups", "blk"), None, None),
        P(("groups", "blk")),
        P(("groups", "blk")),
        P(("groups", "blk"), None),
        P("groups"),
        P(("groups", "blk"), None),
    )
    return jax.shard_map(
        per_device,
        mesh=mesh,
        in_specs=placed,
        out_specs=(P(("groups", "blk")), P(("groups", "blk"))),
        check_vma=False,
    )
```

```python
import jax
import jax.numpy as jnp
from jax import lax
from jax.experimental import pallas as pl
from jax.experimental.pallas import tpu as pltpu
from jax.sharding import PartitionSpec as P

PIECES = 4
AHEAD = 4
PLANE = 4
GROUP = 4

OWN, CORE, SIDE, CORE_SIDE, FIRST, SECOND, DIAG, CORE_DIAG, CORE_PLANE = range(9)
SLOTS = 9


def kernel(
    in_hbm, out_hbm, counts_ref, tclus_ref, q_hbm, qclus_ref, mask_ref,
    train_ref, query_ref,
    in_raw, out_raw, in_f32, out_f32, sketch, blocks, qacc, tacc, qout, qin,
    load_sem, own_sem, send_sem, recv_sem, back_send, back_recv,
):
    n = lax.axis_size("blk")
    b = lax.axis_index("blk")
    place = lax.rem(b, PLANE)
    side = place // 2
    core = lax.rem(place, 2)
    slots, rin, rows = in_f32.shape
    rout = out_f32.shape[1]
    tile = query_ref.shape[1]
    band = mask_ref.shape[1]
    reach = (band - 1) // 2
    width = rin * rout
    piece = tile // PIECES
    scale = 1.0 / width**0.5 / 32.0

    to_core = b + 1 - 2 * core
    to_side = b + 2 - 4 * side
    above = lax.rem(b + PLANE, n)
    below = lax.rem(b + n - PLANE, n)
    to_first = side * above + (1 - side) * below
    to_second = side * below + (1 - side) * above
    offsets = {
        OWN: 0,
        CORE: 1 - 2 * core,
        SIDE: 2 - 4 * side,
        CORE_SIDE: 3 - 2 * place,
        FIRST: 4 - 8 * side,
        SECOND: 8 * side - 4,
        DIAG: 4 * side - 2,
        CORE_DIAG: 8 * side - 1 - 2 * place,
        CORE_PLANE: 6 * core - 3,
    }

    load_in = pltpu.make_async_copy(in_hbm, in_raw, load_sem.at[0])
    load_out = pltpu.make_async_copy(out_hbm, out_raw, load_sem.at[1])
    load_in.start()
    load_out.start()

    barrier = pltpu.get_barrier_semaphore()
    for step in range(1, reach + 1):
        for other in (lax.rem(b + step, n), lax.rem(b + n - step, n)):
            pl.semaphore_signal(
                barrier, inc=1, device_id={"blk": other}, device_id_type=pl.DeviceIdType.MESH
            )
    pl.semaphore_wait(barrier, 2 * reach)

    def own(h):
        return q_hbm.at[pl.ds(h * piece, piece), :]

    def send(src, slot, h, device):
        return pltpu.make_async_remote_copy(
            src_ref=src,
            dst_ref=blocks.at[h, slot],
            send_sem=send_sem.at[slot, h],
            recv_sem=recv_sem.at[slot, h],
            device_id={"blk": device},
            device_id_type=pl.DeviceIdType.MESH,
        )

    pieces = range(PIECES)
    first = [send(own(h), FIRST, h, to_first) for h in pieces]
    aside = [send(own(h), SIDE, h, to_side) for h in pieces]
    twin = [send(own(h), CORE, h, to_core) for h in pieces]
    second = [send(own(h), SECOND, h, to_second) for h in pieces]
    diag = [send(blocks.at[h, FIRST], DIAG, h, to_side) for h in pieces]
    twin_side = [send(blocks.at[h, SIDE], CORE_SIDE, h, to_core) for h in pieces]
    twin_diag = [send(blocks.at[h, DIAG], CORE_DIAG, h, to_core) for h in pieces]
    plane_first = [send(blocks.at[h, FIRST], CORE_PLANE, h, to_core) for h in pieces]
    plane_second = [send(blocks.at[h, SECOND], CORE_PLANE, h, to_core) for h in pieces]
    mine = [pltpu.make_async_copy(own(h), blocks.at[h, OWN], own_sem.at[h]) for h in pieces]
    for h in pieces:
        first[h].start()
        aside[h].start()
    for h in pieces:
        twin[h].start()
        mine[h].start()

    load_in.wait()
    load_out.wait()
    counts = counts_ref[...]

    @pl.loop(0, slots)
    def _(t):
        live = counts > t
        value = in_raw[t].astype(jnp.float32)
        in_f32[t] = jnp.where(live, value, 0.0)
        out_f32[t] = out_raw[t].astype(jnp.float32)

    @pl.loop(0, rows // 128)
    def _(chunk):
        lanes = pl.ds(pl.multiple_of(chunk * 128, 128), 128)

        @pl.loop(0, rin // 8)
        def _(group):
            eight = pl.ds(pl.multiple_of(group * 8, 8), 8)
            for low in range(0, 8, GROUP):
                sums = [None] * GROUP
                for t in range(slots):
                    right = out_f32[t, :, lanes]
                    left = in_f32[t, eight, lanes]
                    for g in range(GROUP):
                        row = left[low + g : low + g + 1]
                        term = row * right
                        sums[g] = term if t == 0 else sums[g] + term
                for g in range(GROUP):
                    at = pl.multiple_of(group * (8 * rout) + (low + g) * rout, rout)
                    sketch[pl.ds(at, rout), lanes] = sums[g].astype(jnp.bfloat16)

    for h in pieces:
        first[h].wait_send()
    for h in pieces[:AHEAD]:
        second[h].start()
    for h in pieces:
        first[h].wait_recv()
        if h < AHEAD:
            diag[h].start()

        @pl.when(side == core)
        def _(h=h):
            plane_first[h].start()

        aside[h].wait_recv()
        twin_side[h].start()

    tacc[...] = jnp.zeros_like(tacc)
    qacc[...] = jnp.zeros_like(qacc)

    def score(parts, low, high):
        clusters = {}
        for slot in range(low, high):
            source = lax.rem(b + offsets[slot] + n, n)
            row = qclus_ref[source].astype(jnp.float32)
            full = jnp.transpose(jnp.broadcast_to(row, (tile, tile)))
            for h in parts:
                clusters[h, slot] = full[h * piece : (h + 1) * piece]

        @pl.loop(0, rows // 256)
        def _(step):
            lanes = pl.ds(pl.multiple_of(step * 256, 256), 256)
            query = jnp.concatenate(
                [blocks[h, low:high].reshape((high - low) * piece, width) for h in parts]
            )
            dots = jnp.dot(query, sketch[:, lanes], preferred_element_type=jnp.float32)
            for part in range(2):
                tile_lanes = pl.ds(pl.multiple_of(step * 256 + part * 128, 128), 128)
                tclus = tclus_ref[:, tile_lanes].astype(jnp.float32)
                total = tacc[:, tile_lanes]
                for slot in range(low, high):
                    open_tile = mask_ref[step * 2 + part, offsets[slot] + reach]
                    wanted = jnp.where(open_tile > 0, tclus, -1.0)
                    for i, h in enumerate(parts):
                        at = (i * (high - low) + slot - low) * piece
                        got = dots[at : at + piece, part * 128 : part * 128 + 128]
                        same = clusters[h, slot] == wanted
                        got = jnp.where(same, jnp.maximum(got, 0.0), 0.0)
                        total = total + jnp.sum(got.reshape(piece // 8, 8, 128), axis=0)
                        qacc[slot, h * piece : (h + 1) * piece, :] += got
                tacc[:, tile_lanes] = total

    def back(slot):
        return pltpu.make_async_remote_copy(
            src_ref=qout.at[slot],
            dst_ref=qin.at[offsets[slot] + reach],
            send_sem=back_send.at[slot],
            recv_sem=back_recv.at[offsets[slot] + reach],
            device_id={"blk": lax.rem(b + offsets[slot] + n, n)},
            device_id_type=pl.DeviceIdType.MESH,
        )

    def give_back(low, high):
        for slot in range(low, high):
            qout[slot] = jnp.sum(jnp.transpose(qacc[slot]), axis=0, keepdims=True)
            if slot != OWN:
                back(slot).start()

    for parts in (pieces[: PIECES // 2], pieces[PIECES // 2 :]):
        for h in parts:
            mine[h].wait()
            twin[h].wait_recv()
            twin_side[h].wait_recv()
        score(parts, OWN, SECOND)
    give_back(OWN, SECOND)

    for h in pieces:
        diag[h].wait_recv()
        twin_diag[h].start()
        second[h].wait_recv()

        @pl.when(side != core)
        def _(h=h):
            plane_second[h].start()

        if h + AHEAD < PIECES:
            second[h].wait_send()
            second[h + AHEAD].start()
            diag[h].wait_send()
            diag[h + AHEAD].start()
        twin_diag[h].wait_recv()
        plane_first[h].wait_recv()
        score((h,), SECOND, SLOTS)
    give_back(SECOND, SLOTS)

    train_ref[...] = jnp.sum(tacc[...], axis=0, keepdims=True) * scale
    total = qout[OWN]
    for column in range(band):
        if column != reach:
            pltpu.make_async_remote_copy(
                src_ref=qout.at[0],
                dst_ref=qin.at[column],
                send_sem=back_send.at[0],
                recv_sem=back_recv.at[column],
                device_id={"blk": to_core},
                device_id_type=pl.DeviceIdType.MESH,
            ).wait_recv()
            total = total + qin[column]
    query_ref[...] = total * scale

    for h in pieces:
        for copy in (aside, twin, twin_side, twin_diag, plane_first):
            copy[h].wait_send()
    for h in pieces[max(PIECES - AHEAD, 0) :]:
        second[h].wait_send()
        diag[h].wait_send()
    for slot in range(1, SLOTS):
        back(slot).wait_send()


def per_device(
    in_factors, out_factors, token_counts, train_cluster, queries, query_cluster, pair_mask
):
    rows, slots, rin = in_factors.shape
    rout = out_factors.shape[2]
    tile, width = queries.shape
    nblocks = lax.axis_size("blk")
    band = pair_mask.shape[1]
    piece = tile // PIECES
    vmem = pl.BlockSpec(memory_space=pltpu.VMEM)
    anywhere = pl.BlockSpec(memory_space=pl.ANY)
    train, query = pl.pallas_call(
        kernel,
        out_shape=(
            jax.ShapeDtypeStruct((1, rows), jnp.float32),
            jax.ShapeDtypeStruct((1, tile), jnp.float32),
        ),
        in_specs=[
            anywhere, anywhere, vmem, vmem, anywhere, vmem,
            pl.BlockSpec(memory_space=pltpu.SMEM),
        ],
        out_specs=(vmem, vmem),
        scratch_shapes=[
            pltpu.VMEM((slots, rin, rows), jnp.bfloat16),
            pltpu.VMEM((slots, rout, rows), jnp.bfloat16),
            pltpu.VMEM((slots, rin, rows), jnp.float32),
            pltpu.VMEM((slots, rout, rows), jnp.float32),
            pltpu.VMEM((width, rows), jnp.bfloat16),
            pltpu.VMEM((PIECES, SLOTS, piece, width), jnp.bfloat16),
            pltpu.VMEM((SLOTS, tile, 128), jnp.float32),
            pltpu.VMEM((8, rows), jnp.float32),
            pltpu.VMEM((SLOTS, 1, tile), jnp.float32),
            pltpu.VMEM((band, 1, tile), jnp.float32),
            pltpu.SemaphoreType.DMA((2,)),
            pltpu.SemaphoreType.DMA((PIECES,)),
            pltpu.SemaphoreType.DMA((SLOTS, PIECES)),
            pltpu.SemaphoreType.DMA((SLOTS, PIECES)),
            pltpu.SemaphoreType.DMA((SLOTS,)),
            pltpu.SemaphoreType.DMA((band,)),
        ],
        compiler_params=pltpu.CompilerParams(
            collective_id=0, has_side_effects=True, vmem_limit_bytes=56 * 2**20
        ),
        name="score_blocks",
    )(
        jnp.transpose(in_factors, (1, 2, 0)),
        jnp.transpose(out_factors, (1, 2, 0)),
        token_counts.reshape(1, rows),
        train_cluster.reshape(1, rows),
        queries,
        query_cluster.reshape(nblocks, 1, tile),
        pair_mask,
    )
    return train.reshape(rows), query.reshape(tile)


def solution(mesh):
    placed = (
        P(("groups", "blk"), None, None),
        P(("groups", "blk"), None, None),
        P(("groups", "blk")),
        P(("groups", "blk")),
        P(("groups", "blk"), None),
        P("groups"),
        P(("groups", "blk"), None),
    )
    return jax.shard_map(
        per_device,
        mesh=mesh,
        in_specs=placed,
        out_specs=(P(("groups", "blk")), P(("groups", "blk"))),
        check_vma=False,
    )
```

```python
import jax
import jax.numpy as jnp
from jax import lax
from jax.experimental import pallas as pl
from jax.experimental.pallas import tpu as pltpu
from jax.sharding import PartitionSpec as P

SHARES = (2, 2, 2, 2)
PIECES = len(SHARES)
PLANE = 4
GROUP = 4

OWN, CORE, SIDE, CORE_SIDE, FIRST, SECOND, DIAG, CORE_DIAG, CORE_PLANE = range(9)
SLOTS = 9


def kernel(
    in_hbm, out_hbm, counts_ref, tclus_ref, q_hbm, qclus_ref, mask_ref,
    train_ref, query_ref,
    in_raw, out_raw, in_f32, out_f32, sketch, blocks, qacc, tacc, qout, qin,
    load_sem, own_sem, send_sem, recv_sem, back_send, back_recv,
):
    n = lax.axis_size("blk")
    b = lax.axis_index("blk")
    place = lax.rem(b, PLANE)
    side = place // 2
    core = lax.rem(place, 2)
    slots, rin, rows = in_f32.shape
    rout = out_f32.shape[1]
    tile = query_ref.shape[1]
    band = mask_ref.shape[1]
    reach = (band - 1) // 2
    width = rin * rout
    sizes = [share * (tile // 8) for share in SHARES]
    starts = [sum(sizes[:h]) for h in range(PIECES)]
    scale = 1.0 / width**0.5 / 32.0

    to_core = b + 1 - 2 * core
    to_side = b + 2 - 4 * side
    above = lax.rem(b + PLANE, n)
    below = lax.rem(b + n - PLANE, n)
    to_first = side * above + (1 - side) * below
    to_second = side * below + (1 - side) * above
    offsets = {
        OWN: 0,
        CORE: 1 - 2 * core,
        SIDE: 2 - 4 * side,
        CORE_SIDE: 3 - 2 * place,
        FIRST: 4 - 8 * side,
        SECOND: 8 * side - 4,
        DIAG: 4 * side - 2,
        CORE_DIAG: 8 * side - 1 - 2 * place,
        CORE_PLANE: 6 * core - 3,
    }

    load_in = pltpu.make_async_copy(in_hbm, in_raw, load_sem.at[0])
    load_out = pltpu.make_async_copy(out_hbm, out_raw, load_sem.at[1])
    load_in.start()
    load_out.start()

    barrier = pltpu.get_barrier_semaphore()
    for step in range(1, reach + 1):
        for other in (lax.rem(b + step, n), lax.rem(b + n - step, n)):
            pl.semaphore_signal(
                barrier, inc=1, device_id={"blk": other}, device_id_type=pl.DeviceIdType.MESH
            )
    pl.semaphore_wait(barrier, 2 * reach)

    def own(h):
        return q_hbm.at[pl.ds(starts[h], sizes[h]), :]

    def held(h, slot):
        return blocks.at[pl.ds(SLOTS * starts[h] + slot * sizes[h], sizes[h]), :]

    def send(src, slot, h, device):
        return pltpu.make_async_remote_copy(
            src_ref=src,
            dst_ref=held(h, slot),
            send_sem=send_sem.at[slot, h],
            recv_sem=recv_sem.at[slot, h],
            device_id={"blk": device},
            device_id_type=pl.DeviceIdType.MESH,
        )

    pieces = range(PIECES)
    first = [send(own(h), FIRST, h, to_first) for h in pieces]
    aside = [send(own(h), SIDE, h, to_side) for h in pieces]
    twin = [send(own(h), CORE, h, to_core) for h in pieces]
    second = [send(own(h), SECOND, h, to_second) for h in pieces]
    diag = [send(held(h, FIRST), DIAG, h, to_side) for h in pieces]
    twin_side = [send(held(h, SIDE), CORE_SIDE, h, to_core) for h in pieces]
    twin_diag = [send(held(h, DIAG), CORE_DIAG, h, to_core) for h in pieces]
    plane_first = [send(held(h, FIRST), CORE_PLANE, h, to_core) for h in pieces]
    plane_second = [send(held(h, SECOND), CORE_PLANE, h, to_core) for h in pieces]
    mine = [pltpu.make_async_copy(own(h), held(h, OWN), own_sem.at[h]) for h in pieces]
    for h in pieces:
        first[h].start()
        aside[h].start()
    for h in pieces:
        twin[h].start()
        mine[h].start()

    load_in.wait()
    load_out.wait()
    counts = counts_ref[...]

    @pl.loop(0, slots)
    def _(t):
        live = counts > t
        value = in_raw[t].astype(jnp.float32)
        in_f32[t] = jnp.where(live, value, 0.0)
        out_f32[t] = out_raw[t].astype(jnp.float32)

    @pl.loop(0, rows // 128)
    def _(chunk):
        lanes = pl.ds(pl.multiple_of(chunk * 128, 128), 128)

        @pl.loop(0, rin // 8)
        def _(group):
            eight = pl.ds(pl.multiple_of(group * 8, 8), 8)
            for low in range(0, 8, GROUP):
                sums = [None] * GROUP
                for t in range(slots):
                    right = out_f32[t, :, lanes]
                    left = in_f32[t, eight, lanes]
                    for g in range(GROUP):
                        row = left[low + g : low + g + 1]
                        term = row * right
                        sums[g] = term if t == 0 else sums[g] + term
                for g in range(GROUP):
                    at = pl.multiple_of(group * (8 * rout) + (low + g) * rout, rout)
                    sketch[pl.ds(at, rout), lanes] = sums[g].astype(jnp.bfloat16)

    for h in pieces:
        first[h].wait_send()
    for h in pieces:
        second[h].start()
    for h in pieces:
        first[h].wait_recv()
        diag[h].start()

        @pl.when(side == core)
        def _(h=h):
            plane_first[h].start()

        aside[h].wait_recv()
        twin_side[h].start()

    tacc[...] = jnp.zeros_like(tacc)
    qacc[...] = jnp.zeros_like(qacc)

    def score(parts, low, high):
        clusters = {}
        for slot in range(low, high):
            source = lax.rem(b + offsets[slot] + n, n)
            row = qclus_ref[source].astype(jnp.float32)
            full = jnp.transpose(jnp.broadcast_to(row, (tile, tile)))
            for h in parts:
                clusters[h, slot] = full[starts[h] : starts[h] + sizes[h]]

        @pl.loop(0, rows // 256)
        def _(step):
            lanes = pl.ds(pl.multiple_of(step * 256, 256), 256)
            query = jnp.concatenate(
                [
                    blocks[SLOTS * starts[h] + low * sizes[h] : SLOTS * starts[h] + high * sizes[h]]
                    for h in parts
                ]
            )
            dots = jnp.dot(query, sketch[:, lanes], preferred_element_type=jnp.float32)
            for part in range(2):
                tile_lanes = pl.ds(pl.multiple_of(step * 256 + part * 128, 128), 128)
                tclus = tclus_ref[:, tile_lanes].astype(jnp.float32)
                total = tacc[:, tile_lanes]
                for slot in range(low, high):
                    open_tile = mask_ref[step * 2 + part, offsets[slot] + reach]
                    wanted = jnp.where(open_tile > 0, tclus, -1.0)
                    for h in parts:
                        before = (starts[h] - starts[parts[0]]) * (high - low)
                        at = before + (slot - low) * sizes[h]
                        got = dots[at : at + sizes[h], part * 128 : part * 128 + 128]
                        same = clusters[h, slot] == wanted
                        got = jnp.where(same, jnp.maximum(got, 0.0), 0.0)
                        total = total + jnp.sum(got.reshape(sizes[h] // 8, 8, 128), axis=0)
                        qacc[slot, starts[h] : starts[h] + sizes[h], :] += got
                tacc[:, tile_lanes] = total

    def back(slot):
        return pltpu.make_async_remote_copy(
            src_ref=qout.at[slot],
            dst_ref=qin.at[offsets[slot] + reach],
            send_sem=back_send.at[slot],
            recv_sem=back_recv.at[offsets[slot] + reach],
            device_id={"blk": lax.rem(b + offsets[slot] + n, n)},
            device_id_type=pl.DeviceIdType.MESH,
        )

    def give_back(low, high):
        for slot in range(low, high):
            qout[slot] = jnp.sum(jnp.transpose(qacc[slot]), axis=0, keepdims=True)
            if slot != OWN:
                back(slot).start()

    for parts in (pieces[: PIECES // 2], pieces[PIECES // 2 :]):
        for h in parts:
            mine[h].wait()
            twin[h].wait_recv()
            twin_side[h].wait_recv()
        score(parts, OWN, SECOND)
    give_back(OWN, SECOND)

    for parts in (pieces[:2], pieces[2:3], pieces[3:]):
        for h in parts:
            diag[h].wait_recv()
            twin_diag[h].start()
            second[h].wait_recv()

            @pl.when(side != core)
            def _(h=h):
                plane_second[h].start()

        for h in parts:
            twin_diag[h].wait_recv()
            plane_first[h].wait_recv()
        score(parts, SECOND, SLOTS)
    give_back(SECOND, SLOTS)

    train_ref[...] = jnp.sum(tacc[...], axis=0, keepdims=True) * scale
    total = qout[OWN]
    for column in range(band):
        if column != reach:
            pltpu.make_async_remote_copy(
                src_ref=qout.at[0],
                dst_ref=qin.at[column],
                send_sem=back_send.at[0],
                recv_sem=back_recv.at[column],
                device_id={"blk": to_core},
                device_id_type=pl.DeviceIdType.MESH,
            ).wait_recv()
            total = total + qin[column]
    query_ref[...] = total * scale

    for h in pieces:
        for copy in (aside, twin, second, diag, twin_side, twin_diag, plane_first):
            copy[h].wait_send()
    for slot in range(1, SLOTS):
        back(slot).wait_send()


def per_device(
    in_factors, out_factors, token_counts, train_cluster, queries, query_cluster, pair_mask
):
    rows, slots, rin = in_factors.shape
    rout = out_factors.shape[2]
    tile, width = queries.shape
    nblocks = lax.axis_size("blk")
    band = pair_mask.shape[1]
    vmem = pl.BlockSpec(memory_space=pltpu.VMEM)
    anywhere = pl.BlockSpec(memory_space=pl.ANY)
    train, query = pl.pallas_call(
        kernel,
        out_shape=(
            jax.ShapeDtypeStruct((1, rows), jnp.float32),
            jax.ShapeDtypeStruct((1, tile), jnp.float32),
        ),
        in_specs=[
            anywhere, anywhere, vmem, vmem, anywhere, vmem,
            pl.BlockSpec(memory_space=pltpu.SMEM),
        ],
        out_specs=(vmem, vmem),
        scratch_shapes=[
            pltpu.VMEM((slots, rin, rows), jnp.bfloat16),
            pltpu.VMEM((slots, rout, rows), jnp.bfloat16),
            pltpu.VMEM((slots, rin, rows), jnp.float32),
            pltpu.VMEM((slots, rout, rows), jnp.float32),
            pltpu.VMEM((width, rows), jnp.bfloat16),
            pltpu.VMEM((SLOTS * tile, width), jnp.bfloat16),
            pltpu.VMEM((SLOTS, tile, 128), jnp.float32),
            pltpu.VMEM((8, rows), jnp.float32),
            pltpu.VMEM((SLOTS, 1, tile), jnp.float32),
            pltpu.VMEM((band, 1, tile), jnp.float32),
            pltpu.SemaphoreType.DMA((2,)),
            pltpu.SemaphoreType.DMA((PIECES,)),
            pltpu.SemaphoreType.DMA((SLOTS, PIECES)),
            pltpu.SemaphoreType.DMA((SLOTS, PIECES)),
            pltpu.SemaphoreType.DMA((SLOTS,)),
            pltpu.SemaphoreType.DMA((band,)),
        ],
        compiler_params=pltpu.CompilerParams(
            collective_id=0, has_side_effects=True, vmem_limit_bytes=56 * 2**20
        ),
        name="score_blocks",
    )(
        jnp.transpose(in_factors, (1, 2, 0)),
        jnp.transpose(out_factors, (1, 2, 0)),
        token_counts.reshape(1, rows),
        train_cluster.reshape(1, rows),
        queries,
        query_cluster.reshape(nblocks, 1, tile),
        pair_mask,
    )
    return train.reshape(rows), query.reshape(tile)


def solution(mesh):
    placed = (
        P(("groups", "blk"), None, None),
        P(("groups", "blk"), None, None),
        P(("groups", "blk")),
        P(("groups", "blk")),
        P(("groups", "blk"), None),
        P("groups"),
        P(("groups", "blk"), None),
    )
    return jax.shard_map(
        per_device,
        mesh=mesh,
        in_specs=placed,
        out_specs=(P(("groups", "blk")), P(("groups", "blk"))),
        check_vma=False,
    )
```
